768 devices in a mesh: dp: 128 (over y, x, z_hi), tensor: 6 (over z_lo, core).
Axes of the slice: x: 4, y: 8, z: 12 (z_hi: 4, z_lo: 3; z = z_hi * 3 + z_lo), core: 2. Of those that a mesh axis runs over, the one named last changes fastest.
Arguments:
- teacher_in: bfloat16 [16384, 1920], P('dp', 'tensor'), may hold values from -3 to 3
- norm_gain: float32 [1920], replicated, may hold values from 0.1 to 1.9
- fc1_weight: bfloat16 [1920, 7680], P(None, 'tensor'), may hold values from -0.125 to 0.125
- fc2_weight: bfloat16 [7680, 1920], P('tensor'), may hold values from -0.0625 to 0.0625
- layer_scale: float32 [1920], P('tensor'), may hold values from 0.5 to 2
- route: int32 [16384], P('dp'), may hold values from 0 to 127, as said below
- student_feat: bfloat16 [16384, 1280], P('dp'), may hold values from -24 to 24
- adaptor_weight: bfloat16 [1280, 1920], P(None, 'tensor'), may hold values from -0.15625 to 0.15625
Outputs:
- adaptor_grad: float32 [1280, 1920], P('dp', 'tensor')
The draws below stay inside these ranges and needn't reach their ends.
Inputs may be any that keep to these rules, and one draw needn't show every extreme that they name: `route`: within each aligned block of 128 tokens every value appears exactly 128 // 128 times.
All inputs are finite; a program needn't handle non-finite values.
Results may differ from the reference program's by a relative error of at most 0.0053.
Values may be sent and summed in bfloat16 or wider, within the bound.
A program may use at most 32 MiB of HBM per device.

```python
import math
import jax
import jax.numpy as jnp
from jax import lax

DT = 1920
FF = 7680
DS = 1280
ROWS = 128
TOKENS = 16384
N_DP = 128


def draw_route(key, part):
    key = jax.random.fold_in(key, 7)
    subkeys = jax.random.split(key, N_DP)
    shuffled = jax.vmap(lambda subkey: jax.random.permutation(subkey, ROWS))(subkeys)
    return (shuffled // (ROWS // N_DP)).reshape(-1).astype(jnp.int32)


def with_spikes(drawn, own_key, source, target, blocks, factor):
    def block_of(position):
        return (jnp.arange(drawn.shape[position]) // (drawn.shape[position] // blocks)).reshape((-1,) + (1,) * (drawn.ndim - 1 - position))

    near = jax.random.permutation(own_key, blocks)[block_of(target)]
    other_side = (block_of(target) + blocks // 2) % blocks
    return jnp.where((block_of(source) == near) | (block_of(source) == other_side), factor * drawn, drawn)


def steps_of(rng, shape, cuts, smallest, largest):
    def one(position, parts):
        heights = jax.random.uniform(jax.random.fold_in(jax.random.fold_in(rng, 6), position), (parts,), jnp.float32, smallest / len(cuts), largest / len(cuts))
        return jnp.repeat(jnp.exp(heights), shape[position] // parts).reshape((-1,) + (1,) * (len(shape) - position - 1))

    factor_of = one(*cuts[0])
    for cut in cuts[1:]:
        factor_of = factor_of * one(*cut)
    return factor_of


def bell_draw(rng, shape, scale, limit, cuts=(), kind=jnp.bfloat16):
    result = scale * jax.random.normal(rng, shape, jnp.float32)
    if cuts:
        result = result * steps_of(rng, shape, cuts, -0.22, 0.18)
    return jnp.clip(result, -limit, limit).astype(kind)


def gaussian_with(key, shape, scale, limit, pieces, heavy, kind=jnp.bfloat16):
    result = scale * jax.random.normal(key, shape, jnp.float32)
    if pieces:
        result = result * steps_of(key, shape, pieces, -0.22, 0.18)
    return jnp.clip(with_spikes(result, jax.random.fold_in(key, 3), *heavy), -limit, limit).astype(kind)


def setup_inputs(seed: int = 0) -> dict:
    seeds = jax.random.split(jax.random.key(seed), 9)
    teacher_in = bell_draw(seeds[0], (TOKENS, DT), 0.5, 3.0, ((0, 128), (1, 6)))
    norm_gain = jnp.clip(1.0 + 0.18 * jax.random.normal(seeds[1], (DT,), jnp.float32), 0.1, 1.9)
    fc1_weight = bell_draw(seeds[2], (DT, FF), DT ** -0.5, 0.125, ((1, 6),))
    fc2_weight = bell_draw(seeds[3], (FF, DT), FF ** -0.5, 0.0625, ((0, 6),))
    layer_scale = jnp.clip(jnp.exp(math.log(2.0) - 1.3862944 * jax.random.uniform(seeds[4], (DT,), jnp.float32) ** steps_of(seeds[4], (DT,), ((0, 6),), -0.2, 0.2)), 0.5, 2.0)
    route = draw_route(jax.random.fold_in(seeds[8], 71), 0)
    student_feat = gaussian_with(seeds[6], (TOKENS, DS), 1.0, 24.0, ((0, 128),), (0, 1, 128, 5.5))
    adaptor_weight = bell_draw(seeds[7], (DS, DT), DS ** -0.5, 0.15625, ((1, 6),))
    return {"teacher_in": teacher_in, "norm_gain": norm_gain, "fc1_weight": fc1_weight, "fc2_weight": fc2_weight, "layer_scale": layer_scale, "route": route, "student_feat": student_feat, "adaptor_weight": adaptor_weight}


def reference(teacher_in, norm_gain, fc1_weight, fc2_weight, layer_scale, route, student_feat, adaptor_weight):
    widened = teacher_in.astype(jnp.float32)
    normed = (widened * lax.rsqrt(lax.optimization_barrier(jnp.mean(widened * widened, axis=1, keepdims=True)) + 1e-06) * norm_gain).astype(jnp.bfloat16)
    hidden = jax.nn.gelu(jnp.dot(normed, fc1_weight, preferred_element_type=jnp.float32), approximate=False).astype(jnp.bfloat16)
    mlp_output = jnp.dot(hidden, fc2_weight, preferred_element_type=jnp.float32)
    feature = (widened + layer_scale * mlp_output).astype(jnp.bfloat16)
    sort_keys = route * TOKENS + jnp.arange(TOKENS, dtype=jnp.int32)
    arrival = jnp.argsort(sort_keys).astype(jnp.int32)
    target = feature[arrival]
    predicted = jnp.dot(student_feat, adaptor_weight, preferred_element_type=jnp.float32)
    target_wide = target.astype(jnp.float32)
    agreement = lax.optimization_barrier(jnp.sum(target_wide * predicted, axis=1))
    target_sq = lax.optimization_barrier(jnp.sum(target_wide * target_wide, axis=1))
    predict_sq = lax.optimization_barrier(jnp.sum(predicted * predicted, axis=1))
    target_norm = jnp.sqrt(target_sq + 1e-06)
    predict_norm = jnp.sqrt(predict_sq + 1e-06)
    cosine = agreement / (target_norm * predict_norm)
    loss_scale = DT / math.sqrt(TOKENS)
    upstream = (-loss_scale * (target_wide / (target_norm * predict_norm)[:, None] - (cosine / (predict_norm * predict_norm))[:, None] * predicted)).astype(jnp.bfloat16)
    return lax.dot_general(student_feat, upstream, (((0,), (0,)), ((), ())), preferred_element_type=jnp.float32)
```

```python
import functools
import math

import jax
import jax.numpy as jnp
from jax import lax
from jax.experimental import pallas as pl
from jax.experimental.pallas import tpu as pltpu
from jax.sharding import PartitionSpec as P

MESH = pl.DeviceIdType.MESH
NY, NX, NZ = 8, 4, 4
LANES = 128


def round_up(value, unit):
    return -(-value // unit) * unit


def place(y, x, z):
    return (y * NX + x) * NZ + z


def dp_peers(y, x, z):
    peers = [place(y, lax.rem(x + k, NX), z) for k in (1, NX - 1)]
    peers += [place(lax.rem(y + k, NY), x, z) for k in range(1, NY)]
    peers += [place(y, x, lax.rem(z + k, NZ)) for k in range(1, NZ)]
    return peers


def nearest_first(count):
    order = []
    for k in range(1, count // 2 + 1):
        order += [k] if 2 * k == count else [k, count - k]
    return order


def grad_kernel(st_ref, u_ref, out_ref, s1, r1, s2, r2, own, ys, yr, yown, zs, zr, send, recv):
    me = lax.axis_index("dp")
    z = lax.rem(me, NZ)
    x = lax.rem(lax.div(me, NZ), NX)
    y = lax.div(me, NZ * NX)
    right, left, across = (lax.rem(x + k, NX) for k in (1, 3, 2))
    rows = out_ref.shape[0]
    span = NZ * rows
    pad = round_up(span, 16)
    tile = zs.shape[2]
    full = NY * span
    chunks = [(0, full, 128), (128, full, 128), (256, full // 2, 64)]

    barrier = pltpu.get_barrier_semaphore()
    peers = dp_peers(y, x, z)
    for peer in peers:
        pl.semaphore_signal(barrier, inc=1, device_id={"dp": peer}, device_id_type=MESH)
    pl.semaphore_wait(barrier, len(peers))

    def copy(c, slot, src, dst, peer):
        return pltpu.make_async_remote_copy(
            src_ref=src, dst_ref=dst, send_sem=send.at[c, slot], recv_sem=recv.at[c, slot],
            device_id={"dp": peer}, device_id_type=MESH,
        )

    started = []

    def product(c, block):
        start, height, width = chunks[c]
        cols = u_ref[:, start : start + width]
        if width == LANES:
            return jnp.dot(st_ref[block], cols, preferred_element_type=jnp.float32)
        zeros = jnp.zeros_like(cols)
        low = jnp.concatenate([cols, zeros], axis=1)
        high = jnp.concatenate([zeros, cols], axis=1)
        return jnp.dot(
            st_ref[block, pl.ds(0, height)], low, preferred_element_type=jnp.float32
        ) + jnp.dot(st_ref[block, pl.ds(height, height)], high, preferred_element_type=jnp.float32)

    def halves(c):
        half = chunks[c][1] // 2
        return pl.ds(0, half), pl.ds(half, half)

    def first_x(c):
        height = chunks[c][1]
        s1[c, pl.ds(0, height)] = product(c, across).astype(jnp.bfloat16)
        out = []
        for side, (part, peer) in enumerate(zip(halves(c), (right, left))):
            out.append(copy(c, side, s1.at[c, part], r1.at[c, part], place(y, peer, z)))
            out[-1].start()
        return out

    def second_x(c, before):
        height = chunks[c][1]
        out = []
        for side, (part, peer) in enumerate(zip(halves(c), (right, left))):
            value = product(c, peer)
            s2[c, side, pl.ds(0, height)] = value.astype(jnp.bfloat16)
            before[side].wait_recv()
            s2[c, side, part] = (
                value[part.start : part.start + part.size] + r1[c, part].astype(jnp.float32)
            ).astype(jnp.bfloat16)
            out.append(
                copy(
                    c, 2 + side, s2.at[c, side, pl.ds(0, height)], r2.at[c, side, pl.ds(0, height)],
                    place(y, peer, z),
                )
            )
            out[-1].start()
        own[c, pl.ds(0, height)] = product(c, x)
        return out

    def send_y(c, before):
        height, width = chunks[c][1:]
        value = own[c, pl.ds(0, height)]
        for side in range(2):
            before[side].wait_recv()
            value += r2[c, side, pl.ds(0, height)].astype(jnp.float32)
        if width == LANES:
            value = value.reshape(NY, span, LANES)
        else:
            value = value.reshape(NY // 2, span, LANES)
            rolled = pltpu.roll(value.reshape(height, LANES), 64, 1).reshape(NY // 2, span, LANES)
            value = jnp.concatenate([value, rolled], axis=0)
        yown[c] = value
        ys[c] = jnp.concatenate(
            [value, jnp.zeros((NY, pad - span, LANES), jnp.float32)], axis=1
        ).astype(jnp.bfloat16)
        out = []
        for k in nearest_first(NY):
            to = lax.rem(y + k, NY)
            out.append((k, copy(c, 3 + k, ys.at[c, to], yr.at[c, k - 1], place(to, x, z))))
            out[-1][1].start()
        return out

    def send_z(c, before):
        total = yown[c, y]
        for k, one in before:
            one.wait_recv()
            total += yr[c, k - 1].astype(jnp.float32)[:span]
        total = jnp.concatenate(
            [total, jnp.zeros((pad - span, LANES), jnp.float32)], axis=0
        ).astype(jnp.bfloat16)
        line = lax.broadcasted_iota(jnp.int32, (NZ * tile, pad), 0)
        wanted = lax.div(line, tile) * rows + lax.rem(line, tile)
        column = lax.broadcasted_iota(jnp.int32, (NZ * tile, pad), 1)
        spread = ((wanted == column) & (lax.rem(line, tile) < rows)).astype(jnp.bfloat16)
        placed = jnp.dot(spread, total, preferred_element_type=jnp.float32)
        zs[c] = placed.astype(jnp.bfloat16).reshape(NZ, tile, LANES)
        out = []
        for k in nearest_first(NZ):
            to = lax.rem(z + k, NZ)
            out.append((k, copy(c, 3 + NY - 1 + k, zs.at[c, to], zr.at[c, k - 1], place(y, x, to))))
            out[-1][1].start()
        return out

    def finish(c, before):
        start, _, width = chunks[c]
        total = zs[c, z].astype(jnp.float32)
        for k, one in before:
            one.wait_recv()
            total += zr[c, k - 1].astype(jnp.float32)
        out_ref[:, start : start + width] = total[:rows, :width]

    order = range(len(chunks))
    stage1 = [first_x(c) for c in order]
    stage2 = [second_x(c, stage1[c]) for c in order]
    stage3 = [send_y(c, stage2[c]) for c in order]
    stage4 = [send_z(c, stage3[c]) for c in order]
    for c in order:
        finish(c, stage4[c])
    for c in order:
        for one in stage1[c] + stage2[c]:
            one.wait_send()
        for _, one in stage3[c] + stage4[c]:
            one.wait_send()


def reduce_grad(st, upstream, rows):
    tile = round_up(rows, 16)
    pad = round_up(NZ * rows, 16)
    full = st.shape[1]
    n = 3
    bf = jnp.bfloat16
    slots = 4 + NY - 1 + NZ - 1
    return pl.pallas_call(
        grad_kernel,
        out_shape=jax.ShapeDtypeStruct((rows, upstream.shape[1]), jnp.float32),
        in_specs=[pl.BlockSpec(memory_space=pltpu.VMEM)] * 2,
        out_specs=pl.BlockSpec(memory_space=pltpu.VMEM),
        scratch_shapes=[
            pltpu.VMEM((n, full, LANES), bf),
            pltpu.VMEM((n, full, LANES), bf),
            pltpu.VMEM((n, 2, full, LANES), bf),
            pltpu.VMEM((n, 2, full, LANES), bf),
            pltpu.VMEM((n, full, LANES), jnp.float32),
            pltpu.VMEM((n, NY, pad, LANES), bf),
            pltpu.VMEM((n, NY - 1, pad, LANES), bf),
            pltpu.VMEM((n, NY, NZ * rows, LANES), jnp.float32),
            pltpu.VMEM((n, NZ, tile, LANES), bf),
            pltpu.VMEM((n, NZ - 1, tile, LANES), bf),
            pltpu.SemaphoreType.DMA((n, slots)),
            pltpu.SemaphoreType.DMA((n, slots)),
        ],
        compiler_params=pltpu.CompilerParams(
            collective_id=0, has_side_effects=True, vmem_limit_bytes=40 << 20
        ),
    )(st, upstream)


def local(
    teacher_in, norm_gain, fc1_weight, fc2_weight, layer_scale, route, student_feat, adaptor_weight
):
    row_count = teacher_in.shape[0]
    dp_devices = lax.axis_size("dp")
    sort_keys = route * row_count + jnp.arange(row_count, dtype=jnp.int32)
    arrival = jnp.argsort(sort_keys)
    gathered = lax.all_gather(teacher_in, "tensor", axis=1, tiled=True)
    widened = gathered.astype(jnp.float32)
    normed = (
        widened * lax.rsqrt(jnp.mean(widened * widened, axis=1, keepdims=True) + 1e-06) * norm_gain
    ).astype(jnp.bfloat16)
    hidden = jax.nn.gelu(
        jnp.dot(normed, fc1_weight, preferred_element_type=jnp.float32), approximate=False
    ).astype(jnp.bfloat16)
    partial_value = jnp.dot(hidden, fc2_weight, preferred_element_type=jnp.float32)
    mlp_output = lax.psum_scatter(partial_value, "tensor", scatter_dimension=1, tiled=True)
    feature = (teacher_in.astype(jnp.float32) + layer_scale * mlp_output).astype(jnp.bfloat16)
    target = lax.all_to_all(feature[arrival], "dp", split_axis=0, concat_axis=0, tiled=True)
    predicted = jnp.dot(student_feat, adaptor_weight, preferred_element_type=jnp.float32)
    target_wide = target.astype(jnp.float32)
    agreement, target_sq, predict_sq = lax.psum(
        (
            jnp.sum(target_wide * predicted, axis=1),
            jnp.sum(target_wide * target_wide, axis=1),
            jnp.sum(predicted * predicted, axis=1),
        ),
        "tensor",
    )
    target_norm = jnp.sqrt(target_sq + 1e-06)
    predict_norm = jnp.sqrt(predict_sq + 1e-06)
    cosine = agreement / (target_norm * predict_norm)
    teacher_width = adaptor_weight.shape[1] * lax.axis_size("tensor")
    loss_scale = teacher_width / math.sqrt(row_count * dp_devices)
    upstream = (
        -loss_scale
        * (
            target_wide / (target_norm * predict_norm)[:, None]
            - (cosine / (predict_norm * predict_norm))[:, None] * predicted
        )
    ).astype(jnp.bfloat16)
    rows = student_feat.shape[1] // dp_devices
    st = student_feat.T.reshape(NY, NX, NZ * rows, row_count)
    st = jnp.swapaxes(st, 0, 1).reshape(NX, NY * NZ * rows, row_count)
    return reduce_grad(st, upstream, rows)


def solution(mesh):
    placed = (
        P("dp", "tensor"),
        P(),
        P(None, "tensor"),
        P("tensor", None),
        P("tensor"),
        P("dp"),
        P("dp", None),
        P(None, "tensor"),
    )
    return jax.shard_map(
        local, mesh=mesh, in_specs=placed, out_specs=P("dp", "tensor"), check_vma=False
    )
```

```python
import functools
import math

import jax
import jax.numpy as jnp
from jax import lax
from jax.experimental import pallas as pl
from jax.experimental.pallas import tpu as pltpu
from jax.sharding import PartitionSpec as P

MESH = pl.DeviceIdType.MESH
NY, NX, NZ = 8, 4, 4
LANES = 128


def round_up(value, unit):
    return -(-value // unit) * unit


def place(y, x, z):
    return (y * NX + x) * NZ + z


def dp_peers(y, x, z):
    peers = [place(y, lax.rem(x + k, NX), z) for k in range(1, NX)]
    peers += [place(lax.rem(y + k, NY), x, z) for k in range(1, NY)]
    peers += [place(y, x, lax.rem(z + k, NZ)) for k in range(1, NZ)]
    return peers


def nearest_first(count):
    order = []
    for k in range(1, count // 2 + 1):
        order += [k] if 2 * k == count else [k, count - k]
    return order


def erf_gelu(value):
    return 0.5 * value * (1.0 + lax.erf(value * (1.0 / math.sqrt(2.0))))


def one_hot(rows, columns, source):
    line = lax.broadcasted_iota(jnp.int32, (rows, columns), 0)
    column = lax.broadcasted_iota(jnp.int32, (rows, columns), 1)
    return (source(line) == column).astype(jnp.bfloat16)


def select_rows(matrix, value):
    return jnp.dot(matrix, value, preferred_element_type=jnp.float32)


def kernel(
    scale, x_hbm, gain_ref, fc1_hbm, fc2_hbm, ls_ref, route_ref, stud_hbm, aw_hbm, out_ref,
    fc1, fc2, aw, xg, acc, mine, pair_s, pair_r, chip_s, chip_r,
    b1, b1s, b2, b2s, sfull, turned, st_ref, pred_ref, stat_s, stat_r, u_ref,
    s1, r1, s2, r2, own, ys, yr, yown, zs, zr,
    send, recv, tsend, trecv, local_sem,
):
    bf, f32 = jnp.bfloat16, jnp.float32
    me = lax.axis_index("dp")
    z = lax.rem(me, NZ)
    x = lax.rem(lax.div(me, NZ), NX)
    y = lax.div(me, NZ * NX)
    right, left, across = (lax.rem(x + k, NX) for k in (1, 3, 2))
    t = lax.axis_index("tensor")
    chip, core = lax.div(t, 2), lax.rem(t, 2)
    twin = chip * 2 + 1 - core
    near = jnp.where(chip == 1, 0, 1)
    far = jnp.where(chip == 2, 0, 2)

    tokens, width = xg.shape[1:]
    half = stud_hbm.shape[1] // 2
    rows = out_ref.shape[0]
    span = NZ * rows
    pad = round_up(span, 16)
    tile = zs.shape[2]
    full = NY * span
    chunks = [(0, full, 128), (128, full, 128), (256, full // 2, 64)]

    loads = []

    def load(slot, src, dst):
        one = pltpu.make_async_copy(src, dst, local_sem.at[slot])
        one.start()
        return one

    load_x = load(0, x_hbm, xg.at[t])
    lanes = pl.ds(pl.multiple_of(core * half, half), half)
    block_rows = NX * NZ

    def student_block(to):
        return stud_hbm.at[pl.ds(pl.multiple_of(to * block_rows, block_rows), block_rows), lanes]

    load_stud = load(1, student_block(y), b1.at[y])
    load_fc1 = load(2, fc1_hbm, fc1)
    load_fc2 = [load(3 + q, fc2_hbm.at[:, pl.ds(q * 2 * width, 2 * width)], fc2.at[q]) for q in range(3)]
    load_aw = load(6, aw_hbm, aw)

    barrier = pltpu.get_barrier_semaphore()
    peers = [{"tensor": lax.rem(t + k, 6)} for k in range(1, 6)]
    peers += [{"dp": peer} for peer in dp_peers(y, x, z)]
    for peer in peers:
        pl.semaphore_signal(barrier, inc=1, device_id=peer, device_id_type=MESH)
    pl.semaphore_wait(barrier, len(peers))

    sent = []

    def remote(slot, src, dst, peer, arrive=None):
        arrive = slot if arrive is None else arrive
        return pltpu.make_async_remote_copy(
            src_ref=src, dst_ref=dst, send_sem=tsend.at[slot], recv_sem=trecv.at[arrive],
            device_id=peer, device_id_type=MESH,
        )

    def begin(one):
        one.start()
        sent.append(one)
        return one

    load_x.wait()
    for slot, to in ((0, far), (1, near)):
        begin(remote(slot, xg.at[t], xg.at[t], {"tensor": to * 2 + core}, chip))
    from_twin = begin(remote(6, xg.at[t], xg.at[t], {"tensor": twin}))

    stage_y = []
    for k in nearest_first(NY):
        to = lax.rem(y + k, NY)
        stage_y.append(begin(remote(
            19 + k, student_block(to), b1.at[y], {"dp": place(to, x, z)}
        )))

    def arrived_y(k):
        origin = lax.rem(y + NY - k, NY)
        return remote(19 + k, b1.at[origin], b1.at[origin], {"dp": place(origin, x, z)})

    squares = []

    def accumulate(source):
        value = xg[source].astype(f32)
        squares.append(jnp.sum(value * value, axis=1, keepdims=True))
        part = jnp.dot(
            (value * gain_ref[source]).astype(bf), fc1[source], preferred_element_type=f32
        )
        if len(squares) == 1:
            acc[...] = part
        else:
            acc[...] += part

    def gathered(source, base, origin):
        return remote(base, xg.at[source], xg.at[source], {"tensor": twin}, base + origin)

    def pass_on(slot, origin):
        source = origin * 2 + core
        gathered(source, 0, origin).wait_recv()
        begin(remote(slot, xg.at[source], xg.at[source], {"tensor": twin}, 3 + origin))

    load_fc1.wait()
    accumulate(t)
    pass_on(2, near)
    from_twin.wait_recv()
    accumulate(twin)
    pass_on(3, far)
    accumulate(near * 2 + core)

    load_stud.wait()
    for k in range(1, NY):
        arrived_y(k).wait_recv()
    count = NY * NX * NZ
    by_x = one_hot(count, count, lambda o: (
        lax.rem(o, NY) * (NX * NZ) + lax.div(o, NY * NZ) * NZ + lax.rem(lax.div(o, NY), NZ)
    ))
    b1s[...] = select_rows(by_x, b1[...].reshape(count, half)).astype(bf).reshape(b1s.shape)
    b2[x] = b1s[x]
    for k in nearest_first(NX):
        to = lax.rem(x + k, NX)
        begin(remote(29 + k, b1s.at[to], b2.at[x], {"dp": place(y, to, z)}))

    accumulate(far * 2 + core)
    gathered(near * 2 + 1 - core, 3, near).wait_recv()
    accumulate(near * 2 + 1 - core)

    for k in range(1, NX):
        origin = lax.rem(x + NX - k, NX)
        remote(29 + k, b2.at[origin], b2.at[origin], {"dp": place(y, origin, z)}).wait_recv()
    by_z = one_hot(count, count, lambda o: (
        lax.rem(lax.div(o, NY), NX) * (NZ * NY) + lax.div(o, NY * NX) * NY + lax.rem(o, NY)
    ))
    b2s[...] = select_rows(by_z, b2[...].reshape(count, half)).astype(bf).reshape(b2s.shape)
    sfull[core, z] = b2s[z]
    for k in nearest_first(NZ):
        to = lax.rem(z + k, NZ)
        begin(remote(32 + k, b2s.at[to], sfull.at[core, z], {"dp": place(y, x, to)}))

    gathered(far * 2 + 1 - core, 3, far).wait_recv()
    accumulate(far * 2 + 1 - core)

    factor = lax.rsqrt(sum(squares) * (1.0 / (6 * width)) + 1e-06)
    hidden = erf_gelu(acc[...] * factor).astype(bf)

    pairs = []
    for one in load_fc2:
        one.wait()
    for slot, q in ((7, far), (8, near), (9, chip)):
        part = jnp.dot(hidden, fc2[q], preferred_element_type=f32)
        low, high = part[:, :width], part[:, width:]
        pair_s[slot - 7] = jnp.where(core == 0, high, low).astype(bf)
        pairs.append(begin(remote(slot, pair_s.at[slot - 7], pair_r.at[slot - 7], {"tensor": twin})))
        mine[slot - 7] = jnp.where(core == 0, low, high)
    for i, q in enumerate((far, near)):
        pairs[i].wait_recv()
        chip_s[i] = (mine[i] + pair_r[i].astype(f32)).astype(bf)
        begin(remote(10 + i, chip_s.at[i], chip_r.at[chip], {"tensor": q * 2 + core}, 10 + chip))

    for k in range(1, NZ):
        origin = lax.rem(z + NZ - k, NZ)
        remote(
            32 + k, sfull.at[core, origin], sfull.at[core, origin], {"dp": place(y, x, origin)}
        ).wait_recv()
    twin_half = begin(remote(13, sfull.at[core], sfull.at[core], {"tensor": twin}))
    slot_of = lax.broadcasted_iota(jnp.int32, (count, tokens), 0)
    owner = (lax.rem(slot_of, NY) * NX + lax.rem(lax.div(slot_of, NY), NX)) * NZ + lax.div(
        slot_of, NY * NX
    )
    chosen = owner == route_ref[...]
    match = chosen.astype(bf)
    match_t = jnp.transpose(chosen.astype(f32)).astype(bf)
    load_aw.wait()

    def student(side):
        value = sfull[side].reshape(count, half)
        ordered = select_rows(match_t, value).astype(bf)
        turned[side] = lax.dot_general(
            value, match, (((0,), (0,)), ((), ())), preferred_element_type=f32
        )
        return jnp.dot(ordered, aw[side], preferred_element_type=f32)

    pred_ref[...] = student(core)
    remote(13, sfull.at[1 - core], sfull.at[1 - core], {"tensor": twin}).wait_recv()
    pred_ref[...] += student(1 - core)
    both = turned[...].reshape(NY, NX, span, tokens)
    for k in range(NX):
        st_ref[k] = both[:, k].reshape(full, tokens).astype(bf)

    predicted = pred_ref[...]
    predict_sq = jnp.sum(predicted * predicted, axis=1, keepdims=True)
    pairs[2].wait_recv()
    mlp = mine[2] + pair_r[2].astype(f32)
    for q in (near, far):
        remote(10, chip_r.at[q], chip_r.at[q], {"tensor": twin}, 10 + q).wait_recv()
        mlp += chip_r[q].astype(f32)
    target = (xg[t].astype(f32) + ls_ref[...] * mlp).astype(bf).astype(f32)

    lane = lax.broadcasted_iota(jnp.int32, (tokens, LANES), 1)
    sums = jnp.where(lane == 0, jnp.sum(target * predicted, axis=1, keepdims=True), 0.0)
    sums = jnp.where(lane == 1, jnp.sum(target * target, axis=1, keepdims=True), sums)
    sums = jnp.where(lane == 2, predict_sq, sums)
    stat_s[...] = jnp.transpose(sums)[:8]
    shared = [
        begin(remote(13 + k, stat_s, stat_r.at[k - 1], {"tensor": lax.rem(t + k, 6)}))
        for k in range(1, 6)
    ]
    total = stat_s[...]
    for k, one in enumerate(shared):
        one.wait_recv()
        total += stat_r[k]
    total = jnp.concatenate([total, jnp.zeros((LANES - 8, tokens), f32)], axis=0)
    columns = jnp.transpose(total)
    agreement, target_sq, predict_sq = (columns[:, i : i + 1] for i in range(3))
    target_norm = jnp.sqrt(target_sq + 1e-06)
    predict_norm = jnp.sqrt(predict_sq + 1e-06)
    cosine = agreement / (target_norm * predict_norm)
    u_ref[...] = (
        -scale
        * (
            target * (1.0 / (target_norm * predict_norm))
            - (cosine / (predict_norm * predict_norm)) * predicted
        )
    ).astype(bf)

    def copy(c, slot, src, dst, peer):
        return pltpu.make_async_remote_copy(
            src_ref=src, dst_ref=dst, send_sem=send.at[c, slot], recv_sem=recv.at[c, slot],
            device_id={"dp": peer}, device_id_type=MESH,
        )

    def product(c, block):
        start, height, width = chunks[c]
        cols = u_ref[:, start : start + width]
        if width == LANES:
            return jnp.dot(st_ref[block], cols, preferred_element_type=jnp.float32)
        zeros = jnp.zeros_like(cols)
        low = jnp.concatenate([cols, zeros], axis=1)
        high = jnp.concatenate([zeros, cols], axis=1)
        return jnp.dot(
            st_ref[block, pl.ds(0, height)], low, preferred_element_type=jnp.float32
        ) + jnp.dot(st_ref[block, pl.ds(height, height)], high, preferred_element_type=jnp.float32)

    def halves(c):
        half = chunks[c][1] // 2
        return pl.ds(0, half), pl.ds(half, half)

    def first_x(c):
        height = chunks[c][1]
        s1[c, pl.ds(0, height)] = product(c, across).astype(jnp.bfloat16)
        out = []
        for side, (part, peer) in enumerate(zip(halves(c), (right, left))):
            out.append(copy(c, side, s1.at[c, part], r1.at[c, part], place(y, peer, z)))
            out[-1].start()
        return out

    def second_x(c, before):
        height = chunks[c][1]
        out = []
        for side, (part, peer) in enumerate(zip(halves(c), (right, left))):
            value = product(c, peer)
            s2[c, side, pl.ds(0, height)] = value.astype(jnp.bfloat16)
            before[side].wait_recv()
            s2[c, side, part] = (
                value[part.start : part.start + part.size] + r1[c, part].astype(jnp.float32)
            ).astype(jnp.bfloat16)
            out.append(
                copy(
                    c, 2 + side, s2.at[c, side, pl.ds(0, height)], r2.at[c, side, pl.ds(0, height)],
                    place(y, peer, z),
                )
            )
            out[-1].start()
        own[c, pl.ds(0, height)] = product(c, x)
        return out

    def send_y(c, before):
        height, width = chunks[c][1:]
        value = own[c, pl.ds(0, height)]
        for side in range(2):
            before[side].wait_recv()
            value += r2[c, side, pl.ds(0, height)].astype(jnp.float32)
        if width == LANES:
            value = value.reshape(NY, span, LANES)
        else:
            value = value.reshape(NY // 2, span, LANES)
            rolled = pltpu.roll(value.reshape(height, LANES), 64, 1).reshape(NY // 2, span, LANES)
            value = jnp.concatenate([value, rolled], axis=0)
        yown[c] = value
        ys[c] = jnp.concatenate(
            [value, jnp.zeros((NY, pad - span, LANES), jnp.float32)], axis=1
        ).astype(jnp.bfloat16)
        out = []
        for k in nearest_first(NY):
            to = lax.rem(y + k, NY)
            out.append((k, copy(c, 3 + k, ys.at[c, to], yr.at[c, k - 1], place(to, x, z))))
            out[-1][1].start()
        return out

    def send_z(c, before):
        total = yown[c, y]
        for k, one in before:
            one.wait_recv()
            total += yr[c, k - 1].astype(jnp.float32)[:span]
        total = jnp.concatenate(
            [total, jnp.zeros((pad - span, LANES), jnp.float32)], axis=0
        ).astype(jnp.bfloat16)
        line = lax.broadcasted_iota(jnp.int32, (NZ * tile, pad), 0)
        wanted = lax.div(line, tile) * rows + lax.rem(line, tile)
        column = lax.broadcasted_iota(jnp.int32, (NZ * tile, pad), 1)
        spread = ((wanted == column) & (lax.rem(line, tile) < rows)).astype(jnp.bfloat16)
        placed = jnp.dot(spread, total, preferred_element_type=jnp.float32)
        zs[c] = placed.astype(jnp.bfloat16).reshape(NZ, tile, LANES)
        out = []
        for k in nearest_first(NZ):
            to = lax.rem(z + k, NZ)
            out.append((k, copy(c, 3 + NY - 1 + k, zs.at[c, to], zr.at[c, k - 1], place(y, x, to))))
            out[-1][1].start()
        return out

    def finish(c, before):
        start, _, width = chunks[c]
        total = zs[c, z].astype(jnp.float32)
        for k, one in before:
            one.wait_recv()
            total += zr[c, k - 1].astype(jnp.float32)
        out_ref[:, start : start + width] = total[:rows, :width]

    order = range(len(chunks))
    stage1 = [first_x(c) for c in order]
    stage2 = [second_x(c, stage1[c]) for c in order]
    stage3 = [send_y(c, stage2[c]) for c in order]
    stage4 = [send_z(c, stage3[c]) for c in order]
    for c in order:
        finish(c, stage4[c])
    for c in order:
        for one in stage1[c] + stage2[c]:
            one.wait_send()
        for _, one in stage3[c] + stage4[c]:
            one.wait_send()

    for one in sent:
        one.wait_send()


def fused(scale, rows, x, gain, fc1, fc2, ls, route, stud, aw):
    bf, f32 = jnp.bfloat16, jnp.float32
    tokens, width = x.shape
    hidden = fc2.shape[0]
    half = stud.shape[1] // 2
    count = NY * NX * NZ
    tile = round_up(rows, 16)
    pad = round_up(NZ * rows, 16)
    full = NY * NZ * rows
    n = 3
    slots = 4 + NY - 1 + NZ - 1
    vmem = pl.BlockSpec(memory_space=pltpu.VMEM)
    hbm = pl.BlockSpec(memory_space=pl.ANY)
    return pl.pallas_call(
        functools.partial(kernel, scale),
        out_shape=jax.ShapeDtypeStruct((rows, width), f32),
        in_specs=[hbm, vmem, hbm, hbm, vmem, vmem, hbm, hbm],
        out_specs=vmem,
        scratch_shapes=[
            pltpu.VMEM((6, width, hidden), bf),
            pltpu.VMEM((3, hidden, 2 * width), bf),
            pltpu.VMEM((2, half, width), bf),
            pltpu.VMEM((6, tokens, width), bf),
            pltpu.VMEM((tokens, hidden), f32),
            pltpu.VMEM((3, tokens, width), f32),
            pltpu.VMEM((3, tokens, width), bf),
            pltpu.VMEM((3, tokens, width), bf),
            pltpu.VMEM((2, tokens, width), bf),
            pltpu.VMEM((3, tokens, width), bf),
            pltpu.VMEM((NY, NX * NZ, half), bf),
            pltpu.VMEM((NX, NZ * NY, half), bf),
            pltpu.VMEM((NX, NZ * NY, half), bf),
            pltpu.VMEM((NZ, NX * NY, half), bf),
            pltpu.VMEM((2, NZ, NX * NY, half), bf),
            pltpu.VMEM((2, half, tokens), f32),
            pltpu.VMEM((NX, full, tokens), bf),
            pltpu.VMEM((tokens, width), f32),
            pltpu.VMEM((8, tokens), f32),
            pltpu.VMEM((5, 8, tokens), f32),
            pltpu.VMEM((tokens, width), bf),
            pltpu.VMEM((n, full, LANES), bf),
            pltpu.VMEM((n, full, LANES), bf),
            pltpu.VMEM((n, 2, full, LANES), bf),
            pltpu.VMEM((n, 2, full, LANES), bf),
            pltpu.VMEM((n, full, LANES), f32),
            pltpu.VMEM((n, NY, pad, LANES), bf),
            pltpu.VMEM((n, NY - 1, pad, LANES), bf),
            pltpu.VMEM((n, NY, NZ * rows, LANES), f32),
            pltpu.VMEM((n, NZ, tile, LANES), bf),
            pltpu.VMEM((n, NZ - 1, tile, LANES), bf),
            pltpu.SemaphoreType.DMA((n, slots)),
            pltpu.SemaphoreType.DMA((n, slots)),
            pltpu.SemaphoreType.DMA((40,)),
            pltpu.SemaphoreType.DMA((40,)),
            pltpu.SemaphoreType.DMA((8,)),
        ],
        compiler_params=pltpu.CompilerParams(
            collective_id=0, has_side_effects=True, vmem_limit_bytes=48 << 20
        ),
    )(x, gain, fc1, fc2, ls, route, stud, aw)


def local(
    teacher_in, norm_gain, fc1_weight, fc2_weight, layer_scale, route, student_feat, adaptor_weight
):
    tokens, width = teacher_in.shape
    features = student_feat.shape[1]
    dp_devices, parts = lax.axis_size("dp"), lax.axis_size("tensor")
    scale = width * parts / math.sqrt(tokens * dp_devices)
    return fused(
        scale,
        features // dp_devices,
        teacher_in,
        norm_gain.reshape(parts, 1, width),
        fc1_weight.reshape(parts, width, fc1_weight.shape[1]),
        fc2_weight,
        layer_scale.reshape(1, width),
        route.reshape(1, tokens),
        student_feat,
        adaptor_weight.reshape(2, features // 2, width),
    )


def solution(mesh):
    placed = (
        P("dp", "tensor"),
        P(),
        P(None, "tensor"),
        P("tensor", None),
        P("tensor"),
        P("dp"),
        P("dp", None),
        P(None, "tensor"),
    )
    return jax.shard_map(
        local, mesh=mesh, in_specs=placed, out_specs=P("dp", "tensor"), check_vma=False
    )
```
